256 devices in a mesh: expert: 64 (over z, y, core), ctx: 4 (over x).
Axes of the slice: x: 4, y: 4, z: 8, core: 2. Of those that a mesh axis runs over, the one named last changes fastest.
Arguments:
- query: bfloat16 [128, 128, 576], P('expert'), may hold values from -72 to 72
- cache: bfloat16 [128, 8192, 576], P('expert', 'ctx'), may hold values from -6 to 6
- lengths: int32 [128], P('expert'), may hold values from 2048 to 8192
- blocks: int32 [128, 32], P('expert'), may hold values from 0 to 127, as said below
- moe_tokens: bfloat16 [1024, 7168], P('expert'), may hold values from -6 to 6
- routes: int32 [1024, 8], P('expert'), may hold values from 0 to 15, all different within a row; in each aligned block of 16 rows (0 to 15, 16 to 31, ...) at most 12 rows name the same one
- route_weights: float32 [1024, 8], P('expert'), may hold values from 0.05 to 0.6
- w_gate: bfloat16 [7168, 32768], P('ctx', 'expert'), may hold values from -0.0625 to 0.0625
- w_up: bfloat16 [7168, 32768], P('ctx', 'expert'), may hold values from -0.0625 to 0.0625
- w_down: bfloat16 [32768, 7168], P('expert', 'ctx'), may hold values from -0.125 to 0.125
Outputs:
- attn_out: bfloat16 [128, 128, 512], P('expert', 'ctx')
- moe_out: bfloat16 [1024, 7168], P('expert')
The draws below stay inside these ranges and needn't reach their ends.
Inputs may be any that keep to these rules, and one draw needn't show every extreme that they name: A sequence's 32 block ids are distinct and ascending, each below the count of blocks that hold its tokens, and the last names the block of its newest token (position lengths - 1). `routes`: each row names 8 different experts; among the rows of one index of expert no expert is named by more than 12 rows, and in some index one is named by exactly 12.
All inputs are finite; a program needn't handle non-finite values.
Results may differ from the reference program's by a relative error of at most 0.0049.
Values may be sent and summed in bfloat16 or wider, within the bound.
A program may use at most 128 MiB of HBM per device.

```python
import math
import jax
import jax.numpy as jnp
import numpy as np
from jax import lax

D = 7168
FF = 2048
H = 128
KV = 512
ROPE = 64
TOPK = 8
QK_DIM = 192
EXPERTS = 16
SEL = 32
BLOCK = 64
LEN = 8192
MOE_ROWS = 16
CAP = 12
ATT_TOTAL = 128
MOE_TOTAL = 1024
N_EXPERT = 64


def plan(key):
    key = jax.random.fold_in(key, 11)
    key_len, key_pick, key_sel = jax.random.split(key, 3)
    lengths = jax.random.randint(key_len, (ATT_TOTAL,), SEL * BLOCK, LEN + 1)
    longest = jax.random.randint(key_pick, (), 0, ATT_TOTAL)
    lengths = jnp.where(jnp.arange(ATT_TOTAL) == longest, LEN, lengths).astype(jnp.int32)
    block_count = LEN // BLOCK
    orders = jax.vmap(lambda row_key: jax.random.permutation(row_key, block_count))(jax.random.split(key_sel, ATT_TOTAL))
    usable = (lengths + BLOCK - 1) // BLOCK
    rank_list = jnp.arange(block_count, dtype=jnp.int32)[None, :]
    newest = usable[:, None] - 1
    ordering = jnp.where(orders == newest, -1, jnp.where(orders < usable[:, None], rank_list, rank_list + block_count))
    picked = jnp.argsort(ordering, axis=1, stable=True)[:, :SEL]
    block_ids = jnp.sort(jnp.take_along_axis(orders, picked, axis=1), axis=1)
    return (lengths, block_ids.astype(jnp.int32))


def draw_lengths(key, part):
    lengths, block_ids = plan(key)
    return lengths


def draw_blocks(key, part):
    lengths, block_ids = plan(key)
    return block_ids


def draw_query(key, part):
    own_key = jax.random.fold_in(key, 3)
    values = jax.random.truncated_normal(own_key, -6.0, 6.0, (ATT_TOTAL, H, KV + ROPE), jnp.float32)
    return values.astype(jnp.bfloat16)


def draw_cache(key, part):
    own_key = jax.random.fold_in(key, 5)
    values = jax.random.truncated_normal(own_key, -6.0, 6.0, (ATT_TOTAL, LEN, KV + ROPE), jnp.float32)
    return values.astype(jnp.bfloat16)


def block_levels(stream_key, extent, cuts, smallest, largest):
    def one(dim, blocks):
        draws = jax.random.uniform(jax.random.fold_in(jax.random.fold_in(stream_key, 6), dim), (blocks,), jnp.float32, smallest / len(cuts), largest / len(cuts))
        return jnp.repeat(jnp.exp(draws), extent[dim] // blocks).reshape((-1,) + (1,) * (len(extent) - dim - 1))

    factor_of = one(*cuts[0])
    for cut in cuts[1:]:
        factor_of = factor_of * one(*cut)
    return factor_of


def shared_out(stream_key, own, number, rows, count, top, limit, slope):
    sequence = jax.random.permutation(stream_key, count)
    packed, usual = load_shares(count, rows * top, limit, slope, True), load_shares(count, rows * top, limit, slope, False)
    places = jnp.arange(count)

    def named(sizes, rotation):
        used = int((sizes > 0).sum())
        fixed = max(1, used // 4)
        moved = fixed + (places - fixed + rotation * (used - fixed)) % max(1, count - fixed)
        return jnp.zeros((count,), jnp.int32).at[sequence[jnp.where(places < fixed, places, moved)]].set(jnp.asarray(sizes, jnp.int32))

    sizes = jnp.where(number % 4 == 0, named(packed, number // 4), named(usual, number - number // 4 - 1))
    mixed = jax.random.permutation(jax.random.fold_in(own, 3), count)
    source_of, taker = mixed[0:count // 2 * 2:2], mixed[1:count // 2 * 2:2]
    margin = jnp.minimum(sizes[source_of] - 1, limit - sizes[taker]) // 2
    margin = jnp.where((source_of == sequence[0]) | (taker == sequence[0]) | (sizes[taker] == 0), 0, jnp.maximum(margin, 0))
    moved = jax.random.randint(jax.random.fold_in(own, 4), (count // 2,), 0, 1 << 20) % (margin + 1)
    sizes = sizes.at[source_of].add(-moved).at[taker].add(moved)
    labels = jnp.searchsorted(jnp.cumsum(sizes), jnp.arange(rows * top), side="right").astype(jnp.int32)
    listing = labels.reshape(top, rows).T
    listing = listing[jax.random.permutation(jax.random.fold_in(own, 1), rows)]
    rotation = jax.random.randint(jax.random.fold_in(own, 2), (rows, 1), 0, top)
    return jnp.take_along_axis(listing, (jnp.arange(top)[None, :] + rotation) % top, axis=1)


def load_shares(count, total, limit, skew, full):
    loads = [(1 << 20) // math.isqrt(standing ** skew) + 1 for standing in range(1, count + 1)]
    largest = limit if full else min(limit, max(-(-total // count), total * loads[0] // sum(loads)))
    least = 1 if total - largest >= count - 1 else 0
    holding, spare = [largest] + [least] * (count - 1), total - largest - least * (count - 1)
    while spare > 0:
        free = [i for i in range(1, count) if holding[i] < largest] or [i for i in range(1, count) if holding[i] < limit]
        whole, left = sum([loads[i] for i in free]), spare
        for i in free:
            addition = min(limit - holding[i], max(1, left * loads[i] // whole), spare)
            holding[i] = holding[i] + addition
            spare = spare - addition
    return np.array(holding)


def centred(rng, dims, scale, bound, pieces=(), kind=jnp.bfloat16):
    gain = block_levels(rng, dims, pieces, -0.22, 0.18) if pieces else 1.0
    array = jax.random.normal(rng, dims, jnp.float32) * scale * gain
    return jnp.minimum(jnp.maximum(array, -bound), bound).astype(kind)


def setup_inputs(seed: int = 0) -> dict:
    arg_keys = jax.random.split(jax.random.key(seed), 11)
    query = draw_query(jax.random.fold_in(arg_keys[10], 71), 0)
    cache = draw_cache(jax.random.fold_in(arg_keys[10], 71), 0)
    lengths = draw_lengths(jax.random.fold_in(arg_keys[10], 71), 0)
    blocks = draw_blocks(jax.random.fold_in(arg_keys[10], 71), 0)
    moe_tokens = centred(arg_keys[4], (MOE_TOTAL, D), 1.0, 6.0, ((0, 64),))
    routes_keys = jax.random.split(jax.random.fold_in(arg_keys[5], 1), MOE_TOTAL // MOE_ROWS)
    routes_turns = jax.random.permutation(jax.random.fold_in(arg_keys[5], 3), MOE_TOTAL // MOE_ROWS)
    routes = jax.vmap(lambda own, number: shared_out(jax.random.fold_in(arg_keys[5], 2), own, number, MOE_ROWS, EXPERTS, TOPK, CAP, 2))(routes_keys, routes_turns).reshape((MOE_TOTAL, TOPK))
    route_weights = jnp.clip(0.05 + 0.55 * jax.random.uniform(arg_keys[6], (MOE_TOTAL, TOPK), jnp.float32) ** block_levels(arg_keys[6], (MOE_TOTAL, TOPK), ((0, 64),), -0.2, 0.2), 0.05, 0.6)
    w_gate = centred(arg_keys[7], (D, EXPERTS * FF), D ** -0.5, 0.0625, ((0, 4), (1, 64)))
    w_up = centred(arg_keys[8], (D, EXPERTS * FF), D ** -0.5, 0.0625, ((0, 4), (1, 64)))
    w_down = centred(arg_keys[9], (EXPERTS * FF, D), FF ** -0.5, 0.125, ((0, 64), (1, 4)))
    return {"query": query, "cache": cache, "lengths": lengths, "blocks": blocks, "moe_tokens": moe_tokens, "routes": routes, "route_weights": route_weights, "w_gate": w_gate, "w_up": w_up, "w_down": w_down}


def attend_row(row_items):
    query_row, cache_row, length, block_ids = row_items
    offsets = jnp.arange(BLOCK, dtype=jnp.int32)
    positions = (block_ids[:, None].astype(jnp.int32) * BLOCK + offsets[None, :]).reshape(-1).astype(jnp.int32)
    key_rows = jnp.take(cache_row, positions, axis=0)
    usable = positions < length
    scores = jnp.dot(query_row, key_rows.T, preferred_element_type=jnp.float32) * (QK_DIM ** -0.5)
    scores = jnp.where(usable[None, :], scores, -jnp.inf)
    peak_score = jnp.max(scores, axis=1, keepdims=True)
    weights = jnp.where(usable[None, :], jnp.exp(scores - peak_score), 0.0)
    weight_sum = jnp.sum(weights, axis=1, keepdims=True)
    latent_rows = key_rows[:, :KV].astype(jnp.float32)
    weighted = jnp.dot(weights, latent_rows, precision=lax.Precision.HIGHEST, preferred_element_type=jnp.float32)
    return (weighted / weight_sum).astype(jnp.bfloat16)


def reference(query, cache, lengths, blocks, moe_tokens, routes, route_weights, w_gate, w_up, w_down):
    attn_out = lax.map(attend_row, (query, cache, lengths, blocks))
    rows_max = min(MOE_TOTAL, N_EXPERT * CAP)

    def one_expert(running, expert_id):
        picked = routes == expert_id
        has_route = jnp.any(picked, axis=1)
        route_mix = jnp.sum(jnp.where(picked, route_weights, 0.0), axis=1)
        row_order = jnp.argsort(jnp.where(has_route, 0, 1).astype(jnp.int32), stable=True)[:rows_max]
        gathered = jnp.take(moe_tokens, row_order, axis=0)
        start = (expert_id * FF).astype(jnp.int32)
        gate_cols = lax.dynamic_slice_in_dim(w_gate, start, FF, 1)
        up_cols = lax.dynamic_slice_in_dim(w_up, start, FF, 1)
        down_rows = lax.dynamic_slice_in_dim(w_down, start, FF, 0)
        gate_sum = jnp.dot(gathered, gate_cols, preferred_element_type=jnp.float32)
        up_sum = jnp.dot(gathered, up_cols, preferred_element_type=jnp.float32)
        activated = (jax.nn.silu(gate_sum) * up_sum).astype(jnp.bfloat16)
        produced = jnp.dot(activated, down_rows, preferred_element_type=jnp.float32)
        running = running.at[row_order].add(produced * jnp.take(route_mix, row_order)[:, None])
        return running, None

    running, unused = lax.scan(one_expert, jnp.zeros((MOE_TOTAL, D), jnp.float32), jnp.arange(EXPERTS, dtype=jnp.int32))
    return attn_out, running.astype(jnp.bfloat16)
```

```python
import jax
import jax.numpy as jnp
from jax import lax
from jax.experimental import pallas as pl
from jax.experimental.pallas import tpu as pltpu
from jax.sharding import PartitionSpec as P

FF = 2048
KV = 512
QK_DIM = 192
EXPERTS = 16
BLOCK = 64
CAP = 12
Z, Y, X = 8, 4, 4
ROWS = 16
QUARTER = 1792
WIDE = QUARTER + 128
UNITS = 512
SLOTS = 192
SHARE = SLOTS // X
SPAN = 2048
HEADS = 128
HEAD_SHARE = HEADS // X
WIDTH = 576
LOW = -1e30
A_CHUNKS = ((0, -1, 1, -2), (2, -3, 3, -4))
B_CHUNKS = ((0, 1), (-1, 2))
F32 = jnp.float32
BF16 = jnp.bfloat16

COPIES = {}


def number(*key):
    return COPIES.setdefault(key, len(COPIES))


for d in (1, 2, 3):
    number("spread_y", d)
    number("slab_y", d)
    number("att", d)
    number("att_top", d)
    number("back_y", d)
    number("last_y", d)
    number("out", d)
    for k in range(4):
        number("sums", k, d)
        number("act", k, d)
for d in range(1, 8):
    number("spread_z", d)
    number("last_z", d)
for s in range(4):
    number("right", s)
    number("left", s)
    number("back_right", s)
    number("back_left", s)
for o in (0, -1, 1, -2, 2, -3, 3, -4):
    number("pass_a", o)
    number("give_a", o)
for o in (0, 1, -1, 2):
    number("pass_b", o)
    number("give_b", o)


def kernel(
    blocks_ref, lengths_ref, routes_ref, route_weights_ref, tokens_hbm, query_hbm, cache_hbm, gate_hbm, up_hbm, down_hbm,
    att_ref, out_ref,
    own, ga, gb, w_gate, w_up, w_down, query, cache,
    att_sum, att_send, att_top, att_got, att_got_top,
    earlier, place, mix, sums, sums_send, sums_got, acts,
    oa, ob, ra, rb, right_send, right_got, left_send, left_got,
    final_a, last_y_got, back_send, back_got, final_b, last_z_send, last_z_got, finals,
    load_sem, send_sem, recv_sem,
):
    index = lax.axis_index("expert")
    x = lax.axis_index("ctx")
    core = lax.rem(index, 2)
    y = lax.rem(index // 2, Y)
    z = index // (2 * Y)
    own_expert = index // (FF // UNITS)
    first, second = core == 0, core == 1

    def at(zz, yy, cc):
        return (zz * (2 * Y) + yy * 2 + cc, x)

    def zo(o):
        return lax.rem(z + o + Z, Z)

    def yo(o):
        return lax.rem(y + o + Y, Y)

    def xo(o):
        return lax.rem(x + o + X, X)

    def copy(key, src, dst, device):
        i = COPIES[key]
        return pltpu.make_async_remote_copy(
            src_ref=src, dst_ref=dst, send_sem=send_sem.at[i], recv_sem=recv_sem.at[i], device_id=device,
            device_id_type=pl.DeviceIdType.MESH,
        )

    to_y = lambda o: at(z, yo(o), core)
    to_z = lambda o: at(zo(o), y, core)
    to_x = lambda o: (index, xo(o))
    sibling = at(z, y, 1 - core)

    def rows16(i):
        return pl.ds(pl.multiple_of(i * ROWS, ROWS), ROWS)

    def load(i, src, dst):
        return pltpu.make_async_copy(src, dst, load_sem.at[i])

    loads = [
        load(0, tokens_hbm.at[:, pl.ds(pl.multiple_of(x * QUARTER, 128), QUARTER)], own.at[:, pl.ds(0, QUARTER)]),
        load(1, query_hbm, query),
        load(2, cache_hbm.at[0], cache.at[0]),
        load(3, cache_hbm.at[1], cache.at[1]),
        load(4, gate_hbm, w_gate),
        load(5, up_hbm, w_up),
        load(6, down_hbm, w_down),
    ]
    for one in loads:
        one.start()

    barrier = pltpu.get_barrier_semaphore()

    def greet(device):
        pl.semaphore_signal(barrier, inc=1, device_id=device, device_id_type=pl.DeviceIdType.MESH)

    for d in (1, 2, 3):
        greet(to_x(d))
        greet(to_y(d))
    greet(sibling)

    @pl.when(first)
    def _():
        greet(to_z(1))
        greet(to_z(-1))

    @pl.when(second)
    def _():
        for d in range(1, Z):
            greet(to_z(d))

    lane = lax.broadcasted_iota(jnp.int32, (ROWS, 128), 1)
    mixing = jnp.zeros((ROWS, 128), F32)
    for k in range(8):
        mixing = jnp.where(lane == routes_ref[:, k : k + 1], route_weights_ref[:, k : k + 1], mixing)
    high = mixing.astype(BF16)
    low = (mixing - high.astype(F32)).astype(BF16)
    low = pltpu.roll(low.astype(F32), EXPERTS, 1)
    own[:, QUARTER:] = (high.astype(F32) + low).astype(BF16)
    row_id = lax.broadcasted_iota(jnp.int32, (256, 256), 0)
    column_id = lax.broadcasted_iota(jnp.int32, (256, 256), 1)
    earlier[...] = jnp.where((row_id // ROWS == column_id // ROWS) & (column_id < row_id), 1.0, 0.0).astype(BF16)
    loads[0].wait()

    @pl.when(first)
    def _():
        ga[z, rows16(y), :] = own[...]
        pl.semaphore_wait(barrier, 9)

    @pl.when(second)
    def _():
        gb[y, rows16(z), :] = own[...]
        pl.semaphore_wait(barrier, 14)

    def spread_y(d):
        return copy(("spread_y", d), own, ga.at[z, rows16(y)], to_y(d))

    def spread_y_in(d):
        return copy(("spread_y", d), own, ga.at[z, rows16(yo(-d))], to_y(d))

    def spread_z(d):
        return copy(("spread_z", d), own, gb.at[y, rows16(z)], to_z(d))

    def spread_z_in(d):
        return copy(("spread_z", d), own, gb.at[y, rows16(zo(-d))], to_z(d))

    def right(s):
        return copy(("right", s), ga.at[zo(-s)], ga.at[zo(-s)], to_z(1))

    def right_in(s):
        return copy(("right", s), ga.at[zo(-s - 1)], ga.at[zo(-s - 1)], to_z(1))

    def left(s):
        return copy(("left", s), ga.at[zo(s)], ga.at[zo(s)], to_z(-1))

    def left_in(s):
        return copy(("left", s), ga.at[zo(s + 1)], ga.at[zo(s + 1)], to_z(-1))

    def pass_a(o):
        return copy(("pass_a", o), ga.at[zo(o)], ga.at[zo(o)], sibling)

    def slab_y(d):
        return copy(("slab_y", d), gb.at[y], gb.at[y], to_y(d))

    def slab_y_in(d):
        return copy(("slab_y", d), gb.at[yo(-d)], gb.at[yo(-d)], to_y(d))

    def pass_b(o):
        return copy(("pass_b", o), gb.at[yo(o)], gb.at[yo(o)], sibling)

    @pl.when(first)
    def _():
        for d in (2, 1, 3):
            spread_y(d).start()

    @pl.when(second)
    def _():
        for d in (4, 3, 5, 2, 6, 1, 7):
            spread_z(d).start()

    def attend(s):
        position = x * SPAN + lax.broadcasted_iota(jnp.int32, (1, SPAN), 1)
        owning = position // BLOCK
        chosen = owning == blocks_ref[s, 0]
        for i in range(1, 32):
            chosen = chosen | (owning == blocks_ref[s, i])
        chosen = chosen & (position < lengths_ref[s])
        scores = lax.dot_general(query[s], cache[s], (((1,), (1,)), ((), ())), preferred_element_type=F32)
        scores = jnp.where(chosen, scores * QK_DIM ** (-0.5), LOW)
        peak = jnp.max(scores, axis=1, keepdims=True)
        weights = jnp.exp(scores - peak)
        total = jnp.sum(weights, axis=1, keepdims=True)
        latent = jnp.dot(weights.astype(BF16), cache[s, :, :KV], preferred_element_type=F32)
        half = lax.broadcasted_iota(jnp.int32, (HEADS, 128), 1) < 64
        top = jnp.where(half, peak, total)
        for i in range(X):
            part = slice(i * HEAD_SHARE, (i + 1) * HEAD_SHARE)
            att_sum[i, s] = latent[part]
            att_send[i, s] = latent[part].astype(BF16)
            att_top[i, s] = top[part]

    def att_copy(d):
        return copy(("att", d), att_send.at[xo(d)], att_got.at[d - 1], to_x(d))

    def att_top_copy(d):
        return copy(("att_top", d), att_top.at[xo(d)], att_got_top.at[d - 1], to_x(d))

    def attend_end():
        for d in (1, 2, 3):
            att_copy(d).wait_recv()
            att_top_copy(d).wait_recv()
        tops = [att_top[x]] + [att_got_top[i] for i in range(3)]
        parts = [att_sum[x]] + [att_got[i].astype(F32) for i in range(3)]
        peaks = [t[:, :, 0:1] for t in tops]
        highest = jnp.maximum(jnp.maximum(peaks[0], peaks[1]), jnp.maximum(peaks[2], peaks[3]))
        factors = [jnp.exp(p - highest) for p in peaks]
        total = sum(f * t[:, :, 64:65] for f, t in zip(factors, tops))
        whole = sum(f * p for f, p in zip(factors, parts))
        att_ref[...] = (whole / total).astype(BF16)

    def slabs(k):
        if k % 2 == 0:
            return [ga.at[zo(o)] for o in A_CHUNKS[k // 2]]
        return [gb.at[yo(o)] for o in B_CHUNKS[k // 2]]

    def chunk(k):
        rows = jnp.concatenate([r[...] for r in slabs(k)], axis=0)
        coefficients = rows[:, QUARTER:].astype(F32)
        lanes = lax.broadcasted_iota(jnp.int32, (256, 128), 1)
        mine = (lanes == own_expert) | (lanes == own_expert + EXPERTS)
        share = jnp.sum(jnp.where(mine, coefficients, 0.0), axis=1, keepdims=True)
        hit = share > 0
        hits = jnp.broadcast_to(jnp.where(hit, 1.0, 0.0), (256, 128)).astype(BF16)
        rank = jnp.dot(earlier[...], hits, preferred_element_type=F32)[:, :1].astype(jnp.int32)
        slot = rank + CAP * (lax.broadcasted_iota(jnp.int32, (256, 1), 0) // ROWS)
        slot = jnp.where(hit, slot, -1)
        placing = jnp.where(slot == lax.broadcasted_iota(jnp.int32, (256, SLOTS), 1), 1.0, 0.0).astype(BF16)
        place[k] = placing
        mix[k] = jnp.broadcast_to(share, (256, 128))
        packed = lax.dot_general(
            placing, rows[:, :QUARTER], (((0,), (0,)), ((), ())), preferred_element_type=F32
        ).astype(BF16)
        for half, weight in enumerate((w_gate, w_up)):
            part = jnp.dot(packed, weight[...], preferred_element_type=F32)
            for i in range(X):
                columns = slice(half * UNITS, (half + 1) * UNITS)
                one = part[i * SHARE : (i + 1) * SHARE]
                sums[k, i, :, columns] = one
                sums_send[k, i, :, columns] = one.astype(BF16)
        for d in (2, 1, 3):
            sums_copy(k, d).start()

    def sums_copy(k, d):
        return copy(("sums", k, d), sums_send.at[k, xo(d)], sums_got.at[k, d - 1], to_x(d))

    def act_copy(k, d):
        return copy(("act", k, d), acts.at[k, x], acts.at[k, x], to_x(d))

    def act_copy_in(k, d):
        return copy(("act", k, d), acts.at[k, xo(-d)], acts.at[k, xo(-d)], to_x(d))

    def activate(k):
        for d in (1, 2, 3):
            sums_copy(k, d).wait_recv()
        both = sums[k, x]
        for i in range(3):
            both = both + sums_got[k, i].astype(F32)
        gate, up = both[:, :UNITS], both[:, UNITS:]
        acts[k, x] = (gate / (1.0 + jnp.exp(-gate)) * up).astype(BF16)
        for d in (2, 1, 3):
            act_copy(k, d).start()

    def give_a(o):
        return copy(("give_a", o), oa.at[zo(o)], ra.at[zo(o)], sibling)

    def give_b(o):
        return copy(("give_b", o), ob.at[yo(o)], rb.at[yo(o)], sibling)

    def finish(k):
        for d in (1, 2, 3):
            act_copy_in(k, d).wait_recv()
        inside = jnp.concatenate([acts[k, i] for i in range(X)], axis=0)
        spread = jnp.dot(place[k], inside, preferred_element_type=F32).astype(BF16)
        result = jnp.dot(spread, w_down[...], preferred_element_type=F32) * mix[k][:, :1]
        if k % 2 == 0:
            for i, o in enumerate(A_CHUNKS[k // 2]):
                oa[zo(o)] = result[i * 64 : (i + 1) * 64]

            @pl.when(second)
            def _():
                for o in A_CHUNKS[k // 2]:
                    give_a(o).start()
        else:
            for i, o in enumerate(B_CHUNKS[k // 2]):
                ob[yo(o)] = result[i * 128 : (i + 1) * 128]

            @pl.when(first)
            def _():
                for o in B_CHUNKS[k // 2]:
                    give_b(o).start()

    loads[1].wait()
    loads[2].wait()
    attend(0)

    @pl.when(first)
    def _():
        for d in (1, 2, 3):
            spread_y_in(d).wait_recv()
        right(0).start()
        left(0).start()
        pass_a(0).start()

    @pl.when(second)
    def _():
        for d in range(1, Z):
            spread_z_in(d).wait_recv()
        for d in (2, 1, 3):
            slab_y(d).start()
        pass_b(0).start()

    loads[3].wait()
    attend(1)
    for d in (2, 1, 3):
        att_copy(d).start()
        att_top_copy(d).start()

    @pl.when(first)
    def _():
        right_in(0).wait_recv()
        left_in(0).wait_recv()
        right(1).start()
        left(1).start()
        pass_a(-1).start()
        pass_a(1).start()
        right_in(1).wait_recv()
        left_in(1).wait_recv()
        right(2).start()
        left(2).start()
        pass_a(-2).start()
        pass_a(2).start()

    @pl.when(second)
    def _():
        for o in A_CHUNKS[0]:
            pass_a(o).wait_recv()

    loads[4].wait()
    loads[5].wait()
    chunk(0)

    @pl.when(first)
    def _():
        right_in(2).wait_recv()
        left_in(2).wait_recv()
        right(3).start()
        pass_a(-3).start()
        pass_a(3).start()
        for o in B_CHUNKS[0]:
            pass_b(o).wait_recv()

    @pl.when(second)
    def _():
        for d in (1, 2, 3):
            slab_y_in(d).wait_recv()
            pass_b({1: -1, 2: 2, 3: 1}[d]).start()

    chunk(1)
    activate(0)

    @pl.when(first)
    def _():
        right_in(3).wait_recv()
        pass_a(-4).start()

    @pl.when(second)
    def _():
        for o in A_CHUNKS[1]:
            pass_a(o).wait_recv()

    chunk(2)
    loads[6].wait()
    finish(0)
    activate(1)

    @pl.when(first)
    def _():
        for o in B_CHUNKS[1]:
            pass_b(o).wait_recv()

    chunk(3)
    activate(2)
    finish(1)
    attend_end()
    activate(3)
    finish(2)
    finish(3)

    def back_right(s):
        return copy(("back_right", s), right_send.at[s], right_got.at[s], to_z(1))

    def back_left(s):
        return copy(("back_left", s), left_send.at[s], left_got.at[s], to_z(-1))

    def back_y(d):
        return copy(("back_y", d), back_send.at[d - 1], back_got.at[d - 1], to_y(d))

    def last_y(d):
        return copy(("last_y", d), final_a.at[yo(d)], last_y_got.at[d - 1], to_y(d))

    def last_z(d):
        return copy(("last_z", d), last_z_send.at[zo(d)], last_z_got.at[d - 1], to_z(d))

    def out_copy(d):
        return copy(("out", d), finals.at[x], finals.at[x], to_x(d))

    def out_copy_in(d):
        return copy(("out", d), finals.at[xo(-d)], finals.at[xo(-d)], to_x(d))

    @pl.when(first)
    def _():
        for o in A_CHUNKS[0] + A_CHUNKS[1]:
            give_a(o).wait_recv()

        def chip(o):
            return oa[zo(o)] + ra[zo(o)]

        right_send[0] = chip(4 - Z).astype(BF16)
        back_right(0).start()
        left_send[0] = chip(-3).astype(BF16)
        back_left(0).start()
        for s in (1, 2, 3):
            back_right(s - 1).wait_recv()
            right_send[s] = (chip(4 - s) + right_got[s - 1].astype(F32)).astype(BF16)
            back_right(s).start()
            if s < 3:
                back_left(s - 1).wait_recv()
                left_send[s] = (chip(s - 3) + left_got[s - 1].astype(F32)).astype(BF16)
                back_left(s).start()
        back_left(2).wait_recv()
        back_right(3).wait_recv()
        whole = chip(0) + right_got[3].astype(F32) + left_got[2].astype(F32)
        for i in range(Y):
            final_a[i] = whole[i * ROWS : (i + 1) * ROWS]
        for d in (2, 1, 3):
            last_y(d).start()
        for d in (1, 2, 3):
            last_y(d).wait_recv()
        finals[x] = (final_a[y] + last_y_got[0] + last_y_got[1] + last_y_got[2]).astype(BF16)

    @pl.when(second)
    def _():
        for o in B_CHUNKS[0] + B_CHUNKS[1]:
            give_b(o).wait_recv()

        def chip(o):
            return ob[yo(o)] + rb[yo(o)]

        for d in (2, 1, 3):
            back_send[d - 1] = chip(d if d < 3 else -1).astype(BF16)
            back_y(d).start()
        for d in (1, 2, 3):
            back_y(d).wait_recv()
        whole = chip(0)
        for i in range(3):
            whole = whole + back_got[i].astype(F32)
        for i in range(Z):
            one = whole[i * ROWS : (i + 1) * ROWS]
            final_b[i] = one
            last_z_send[i] = one.astype(BF16)
        for d in (4, 3, 5, 2, 6, 1, 7):
            last_z(d).start()
        total = final_b[z]
        for d in range(1, Z):
            last_z(d).wait_recv()
            total = total + last_z_got[d - 1].astype(F32)
        finals[x] = total.astype(BF16)

    for d in (2, 1, 3):
        out_copy(d).start()
    for d in (1, 2, 3):
        out_copy_in(d).wait_recv()
    for i in range(X):
        out_ref[:, i * QUARTER : (i + 1) * QUARTER] = finals[i]

    for d in (1, 2, 3):
        att_copy(d).wait_send()
        att_top_copy(d).wait_send()
        out_copy(d).wait_send()
        for k in range(4):
            sums_copy(k, d).wait_send()
            act_copy(k, d).wait_send()

    @pl.when(first)
    def _():
        for d in (1, 2, 3):
            spread_y(d).wait_send()
            last_y(d).wait_send()
        for s in range(4):
            right(s).wait_send()
            back_right(s).wait_send()
            if s < 3:
                left(s).wait_send()
                back_left(s).wait_send()
        for o in A_CHUNKS[0] + A_CHUNKS[1]:
            pass_a(o).wait_send()
        for o in B_CHUNKS[0] + B_CHUNKS[1]:
            give_b(o).wait_send()

    @pl.when(second)
    def _():
        for d in range(1, Z):
            spread_z(d).wait_send()
            last_z(d).wait_send()
        for d in (1, 2, 3):
            slab_y(d).wait_send()
            back_y(d).wait_send()
        for o in B_CHUNKS[0] + B_CHUNKS[1]:
            pass_b(o).wait_send()
        for o in A_CHUNKS[0] + A_CHUNKS[1]:
            give_a(o).wait_send()


def shards(query, cache, lengths, blocks, moe_tokens, routes, route_weights, w_gate, w_up, w_down):
    smem = pl.BlockSpec(memory_space=pltpu.SMEM)
    vmem = pl.BlockSpec(memory_space=pltpu.VMEM)
    hbm = pl.BlockSpec(memory_space=pl.ANY)
    scratch = lambda *shape: pltpu.VMEM(shape, BF16)
    wide = lambda *shape: pltpu.VMEM(shape, F32)
    return pl.pallas_call(
        kernel,
        out_shape=(
            jax.ShapeDtypeStruct((2, HEAD_SHARE, KV), BF16),
            jax.ShapeDtypeStruct((ROWS, X * QUARTER), BF16),
        ),
        in_specs=[smem, smem, vmem, vmem] + [hbm] * 6,
        out_specs=(vmem, vmem),
        scratch_shapes=[
            scratch(ROWS, WIDE),
            scratch(Z, 64, WIDE),
            scratch(Y, 128, WIDE),
            scratch(QUARTER, UNITS),
            scratch(QUARTER, UNITS),
            scratch(UNITS, QUARTER),
            scratch(2, HEADS, WIDTH),
            scratch(2, SPAN, WIDTH),
            wide(X, 2, HEAD_SHARE, KV),
            scratch(X, 2, HEAD_SHARE, KV),
            wide(X, 2, HEAD_SHARE, 128),
            scratch(3, 2, HEAD_SHARE, KV),
            wide(3, 2, HEAD_SHARE, 128),
            scratch(256, 256),
            scratch(4, 256, SLOTS),
            wide(4, 256, 128),
            wide(4, X, SHARE, 2 * UNITS),
            scratch(4, X, SHARE, 2 * UNITS),
            scratch(4, 3, SHARE, 2 * UNITS),
            scratch(4, X, SHARE, UNITS),
            wide(Z, 64, QUARTER),
            wide(Y, 128, QUARTER),
            wide(Z, 64, QUARTER),
            wide(Y, 128, QUARTER),
            scratch(4, 64, QUARTER),
            scratch(4, 64, QUARTER),
            scratch(3, 64, QUARTER),
            scratch(3, 64, QUARTER),
            wide(Y, ROWS, QUARTER),
            wide(3, ROWS, QUARTER),
            scratch(3, 128, QUARTER),
            scratch(3, 128, QUARTER),
            wide(Z, ROWS, QUARTER),
            scratch(Z, ROWS, QUARTER),
            scratch(7, ROWS, QUARTER),
            scratch(X, ROWS, QUARTER),
            pltpu.SemaphoreType.DMA((7,)),
            pltpu.SemaphoreType.DMA((len(COPIES),)),
            pltpu.SemaphoreType.DMA((len(COPIES),)),
        ],
        compiler_params=pltpu.CompilerParams(
            collective_id=0, has_side_effects=True, vmem_limit_bytes=62 * 1024 * 1024
        ),
    )(blocks, lengths, routes, route_weights, moe_tokens, query, cache, w_gate, w_up, w_down)


def solution(mesh):
    return jax.shard_map(
        shards,
        mesh=mesh,
        in_specs=(
            P("expert", None, None),
            P("expert", "ctx", None),
            P("expert"),
            P("expert", None),
            P("expert", None),
            P("expert", None),
            P("expert", None),
            P("ctx", "expert"),
            P("ctx", "expert"),
            P("expert", "ctx"),
        ),
        out_specs=(P("expert", "ctx", None), P("expert", None)),
        check_vma=False,
    )
```

```python
import jax
import jax.numpy as jnp
from jax import lax
from jax.experimental import pallas as pl
from jax.experimental.pallas import tpu as pltpu
from jax.sharding import PartitionSpec as P

FF = 2048
KV = 512
QK_DIM = 192
EXPERTS = 16
BLOCK = 64
CAP = 12
Z, Y, X = 8, 4, 4
ROWS = 16
QUARTER = 1792
WIDE = QUARTER + 128
UNITS = 512
SLOTS = Y * 2 * CAP
SHARE = UNITS // X
SPAN = 2048
HEADS = 128
HEAD_SHARE = HEADS // X
WIDTH = 576
LOW = -1e30
PLANES = (0, 1, -1, 2, -2, 3, -3, 4)
CHUNKS = len(PLANES)
PLACE = {o: k for k, o in enumerate(PLANES)}
CHUNK_ROWS = Y * 2 * ROWS
F32 = jnp.float32
BF16 = jnp.bfloat16

COPIES = {}


def number(*key):
    return COPIES.setdefault(key, len(COPIES))


for d in (1, 2, 3):
    number("att", d)
    number("att_top", d)
    number("out", d)
    for k in range(CHUNKS):
        number("sums", k, d)
        number("act", k, d)
        number("back_y", k, d)
    for o in PLACE:
        number("fan", o, d)
for o in PLACE:
    if o:
        number("spread", o)
        number("last_z", o)
for k in range(CHUNKS):
    number("pass", k)
    number("give", k)


def kernel(
    blocks_ref, lengths_ref, routes_ref, route_weights_ref, tokens_hbm, query_hbm, cache_hbm, gate_hbm, up_hbm, down_hbm,
    att_ref, out_ref,
    own, rows_all, w_gate, w_up, w_down, query, cache,
    att_sum, att_send, att_top, att_got, att_got_top,
    earlier, place, mix, sums, sums_send, sums_got, acts,
    results, given, chips, chips_send, chips_got, final_own, last_send, last_got, finals,
    load_sem, send_sem, recv_sem,
):
    index = lax.axis_index("expert")
    x = lax.axis_index("ctx")
    core = lax.rem(index, 2)
    y = lax.rem(index // 2, Y)
    z = index // (2 * Y)
    own_expert = index // (FF // UNITS)

    def at(zz, yy, cc):
        return (zz * (2 * Y) + yy * 2 + cc, x)

    def zo(o):
        return lax.rem(z + o + Z, Z)

    def yo(o):
        return lax.rem(y + o + Y, Y)

    def xo(o):
        return lax.rem(x + o + X, X)

    def copy(key, src, dst, device):
        i = COPIES[key]
        return pltpu.make_async_remote_copy(
            src_ref=src, dst_ref=dst, send_sem=send_sem.at[i], recv_sem=recv_sem.at[i], device_id=device,
            device_id_type=pl.DeviceIdType.MESH,
        )

    to_y = lambda o: at(z, yo(o), core)
    to_z = lambda o: at(zo(o), y, core)
    to_x = lambda o: (index, xo(o))
    sibling = at(z, y, 1 - core)

    def load(i, src, dst):
        return pltpu.make_async_copy(src, dst, load_sem.at[i])

    loads = [
        load(0, tokens_hbm.at[:, pl.ds(pl.multiple_of(x * QUARTER, 128), QUARTER)], own.at[:, pl.ds(0, QUARTER)]),
        load(1, query_hbm, query),
        load(2, cache_hbm.at[0], cache.at[0]),
        load(3, cache_hbm.at[1], cache.at[1]),
        load(4, gate_hbm, w_gate),
        load(5, up_hbm, w_up),
        load(6, down_hbm, w_down),
    ]
    for one in loads:
        one.start()

    barrier = pltpu.get_barrier_semaphore()

    def greet(device):
        pl.semaphore_signal(barrier, inc=1, device_id=device, device_id_type=pl.DeviceIdType.MESH)

    for d in (1, 2, 3):
        greet(to_x(d))
        greet(to_y(d))
    greet(sibling)

    for d in range(1, Z):
        greet(to_z(d))

    expert_id = lax.broadcasted_iota(jnp.int32, (EXPERTS, ROWS), 0)
    mixing = jnp.zeros((EXPERTS, ROWS), F32)
    for k in range(8):
        mixing = jnp.where(expert_id == routes_ref[k : k + 1, :], route_weights_ref[k : k + 1, :], mixing)
    high = mixing.astype(BF16)
    low = (mixing - high.astype(F32)).astype(BF16)
    to_row = lax.broadcasted_iota(jnp.int32, (EXPERTS, 128), 0)
    to_lane = lax.broadcasted_iota(jnp.int32, (EXPERTS, 128), 1)
    turned = [
        lax.dot_general(
            part, jnp.where(to_lane == to_row + shift, 1.0, 0.0).astype(BF16), (((0,), (0,)), ((), ())),
            preferred_element_type=F32,
        )
        for part, shift in ((high, 0), (low, EXPERTS))
    ]
    own[:, QUARTER:] = (turned[0] + turned[1]).astype(BF16)
    row_id = lax.broadcasted_iota(jnp.int32, (CHUNK_ROWS, CHUNK_ROWS), 0)
    column_id = lax.broadcasted_iota(jnp.int32, (CHUNK_ROWS, CHUNK_ROWS), 1)
    earlier[...] = jnp.where((row_id // ROWS == column_id // ROWS) & (column_id < row_id), 1.0, 0.0).astype(BF16)
    loads[0].wait()

    rows_all[0, y, core] = own[...]
    pl.semaphore_wait(barrier, 14)

    def spread(o):
        k = PLACE[o]
        return copy(("spread", o), own, rows_all.at[k, y, core], to_z(-o))

    def fan(o, d):
        k = PLACE[o]
        return copy(("fan", o, d), rows_all.at[k, y, core], rows_all.at[k, y, core], to_y(d))

    def fan_in(o, d):
        k = PLACE[o]
        return copy(("fan", o, d), rows_all.at[k, yo(-d), core], rows_all.at[k, yo(-d), core], to_y(d))

    def pass_on(k):
        return copy(("pass", k), rows_all.at[k, :, core], rows_all.at[k, :, core], sibling)

    def pass_in(k):
        return copy(("pass", k), rows_all.at[k, :, 1 - core], rows_all.at[k, :, 1 - core], sibling)

    def fan_out(k):
        o = PLANES[k]
        if o:
            spread(o).wait_recv()
        for d in (1, 3, 2):
            fan(o, d).start()

    def gather(k):
        for d in (1, 3, 2):
            fan_in(PLANES[k], d).wait_recv()
        pass_on(k).start()

    fan_out(0)
    spread(1).start()
    spread(-1).start()

    def attend(s):
        position = x * SPAN + lax.broadcasted_iota(jnp.int32, (1, SPAN), 1)
        owning = position // BLOCK
        chosen = owning == blocks_ref[s, 0]
        for i in range(1, 32):
            chosen = chosen | (owning == blocks_ref[s, i])
        chosen = chosen & (position < lengths_ref[s])
        scores = lax.dot_general(query[s], cache[s], (((0,), (0,)), ((), ())), preferred_element_type=F32)
        scores = jnp.where(chosen, scores * QK_DIM ** (-0.5), LOW)
        peak = jnp.max(scores, axis=1, keepdims=True)
        weights = jnp.exp(scores - peak)
        total = jnp.sum(weights, axis=1, keepdims=True)
        latent = lax.dot_general(
            weights.astype(BF16), cache[s, :KV], (((1,), (1,)), ((), ())), preferred_element_type=F32
        )
        half = lax.broadcasted_iota(jnp.int32, (HEADS, 128), 1) < 64
        top = jnp.where(half, peak, total)
        for i in range(X):
            part = slice(i * HEAD_SHARE, (i + 1) * HEAD_SHARE)
            att_sum[i, s] = latent[part]
            att_send[i, s] = latent[part].astype(BF16)
            att_top[i, s] = top[part]

    def att_copy(d):
        return copy(("att", d), att_send.at[xo(d)], att_got.at[d - 1], to_x(d))

    def att_top_copy(d):
        return copy(("att_top", d), att_top.at[xo(d)], att_got_top.at[d - 1], to_x(d))

    def attend_end():
        for d in (1, 2, 3):
            att_copy(d).wait_recv()
            att_top_copy(d).wait_recv()
        tops = [att_top[x]] + [att_got_top[i] for i in range(3)]
        parts = [att_sum[x]] + [att_got[i].astype(F32) for i in range(3)]
        peaks = [t[:, :, 0:1] for t in tops]
        highest = jnp.maximum(jnp.maximum(peaks[0], peaks[1]), jnp.maximum(peaks[2], peaks[3]))
        factors = [jnp.exp(p - highest) for p in peaks]
        total = sum(f * t[:, :, 64:65] for f, t in zip(factors, tops))
        whole = sum(f * p for f, p in zip(factors, parts))
        att_ref[...] = (whole / total).astype(BF16)

    def chunk(k):
        pass_in(k).wait_recv()
        rows = rows_all[k].reshape(CHUNK_ROWS, WIDE)
        coefficients = rows[:, QUARTER:].astype(F32)
        lanes = lax.broadcasted_iota(jnp.int32, (CHUNK_ROWS, 128), 1)
        mine = (lanes == own_expert) | (lanes == own_expert + EXPERTS)
        share = jnp.sum(jnp.where(mine, coefficients, 0.0), axis=1, keepdims=True)
        hit = share > 0
        hits = jnp.broadcast_to(jnp.where(hit, 1.0, 0.0), (CHUNK_ROWS, 128)).astype(BF16)
        rank = jnp.dot(earlier[...], hits, preferred_element_type=F32)[:, :1].astype(jnp.int32)
        slot = rank + CAP * (lax.broadcasted_iota(jnp.int32, (CHUNK_ROWS, 1), 0) // ROWS)
        slot = jnp.where(hit, slot, -1)
        placing = jnp.where(slot == lax.broadcasted_iota(jnp.int32, (CHUNK_ROWS, SLOTS), 1), 1.0, 0.0).astype(BF16)
        place[k] = placing
        mix[k] = jnp.broadcast_to(share, (CHUNK_ROWS, 128))
        packed = lax.dot_general(
            placing, rows[:, :QUARTER], (((0,), (0,)), ((), ())), preferred_element_type=F32
        ).astype(BF16)
        for half, weight in enumerate((w_gate, w_up)):
            part = jnp.dot(packed, weight[...], preferred_element_type=F32)
            for i in range(X):
                one = part[:, i * SHARE : (i + 1) * SHARE]
                sums[k, i, :, half * SHARE : (half + 1) * SHARE] = one
                sums_send[k, i, :, half * SHARE : (half + 1) * SHARE] = one.astype(BF16)
        for d in (1, 3, 2):
            sums_copy(k, d).start()

    def sums_copy(k, d):
        return copy(("sums", k, d), sums_send.at[k, xo(d)], sums_got.at[k, d - 1], to_x(d))

    def act_copy(k, d):
        return copy(("act", k, d), acts.at[k, x], acts.at[k, x], to_x(d))

    def act_copy_in(k, d):
        return copy(("act", k, d), acts.at[k, xo(-d)], acts.at[k, xo(-d)], to_x(d))

    def activate(k):
        for d in (1, 2, 3):
            sums_copy(k, d).wait_recv()
        both = sums[k, x]
        for i in range(3):
            both = both + sums_got[k, i].astype(F32)
        gate, up = both[:, :SHARE], both[:, SHARE:]
        acts[k, x] = (gate / (1.0 + jnp.exp(-gate)) * up).astype(BF16)
        for d in (1, 3, 2):
            act_copy(k, d).start()

    def give(k):
        return copy(("give", k), results.at[k, :, 1 - core], given.at[k], sibling)

    def finish(k):
        for d in (1, 2, 3):
            act_copy_in(k, d).wait_recv()
        inside = jnp.concatenate([acts[k, i] for i in range(X)], axis=1)
        spread_out = jnp.dot(place[k], inside, preferred_element_type=F32).astype(BF16)
        result = jnp.dot(spread_out, w_down[...], preferred_element_type=F32) * mix[k][:, :1]
        results[k] = result.reshape(Y, 2, ROWS, QUARTER)
        give(k).start()

    def back_y(k, d):
        return copy(("back_y", k, d), chips_send.at[k, yo(d)], chips_got.at[k, d - 1], to_y(d))

    def last_z(o):
        k = PLACE[o]
        return copy(("last_z", o), last_send.at[k], last_got.at[k], to_z(o))

    def out_copy(d):
        return copy(("out", d), finals.at[x], finals.at[x], to_x(d))

    def out_copy_in(d):
        return copy(("out", d), finals.at[xo(-d)], finals.at[xo(-d)], to_x(d))

    def return_y(k):
        give(k).wait_recv()
        for j in range(Y):
            one = results[k, j, core] + given[k, j]
            chips[k, j] = one
            chips_send[k, j] = one.astype(BF16)
        for d in (1, 3, 2):
            back_y(k, d).start()

    def return_z(k):
        for d in (1, 3, 2):
            back_y(k, d).wait_recv()
        one = chips[k, y]
        for j in range(3):
            one = one + chips_got[k, j].astype(F32)
        if k:
            last_send[k] = one.astype(BF16)
            last_z(PLANES[k]).start()
        else:
            final_own[...] = one

    def spread_next(sent, following):
        for o in sent:
            spread(o).wait_send()
        for o in following:
            spread(o).start()

    loads[1].wait()
    loads[2].wait()
    attend(0)
    spread_next((1, -1), (2, -2))
    fan_out(1)
    fan_out(2)
    loads[3].wait()
    attend(1)
    for d in (1, 3, 2):
        att_copy(d).start()
        att_top_copy(d).start()
    spread_next((2, -2), (3, -3))
    gather(0)
    loads[4].wait()
    loads[5].wait()
    for t in range(CHUNKS + 7):
        if t + 3 < CHUNKS:
            fan_out(t + 3)
        if t == 0:
            spread_next((3, -3), (4,))
        if t + 1 < CHUNKS:
            gather(t + 1)
        if t < CHUNKS:
            chunk(t)
        if t == 3:
            loads[6].wait()
        if 0 <= t - 2 < CHUNKS:
            activate(t - 2)
        if 0 <= t - 4 < CHUNKS:
            finish(t - 4)
        if 0 <= t - 5 < CHUNKS:
            return_y(t - 5)
        if 0 <= t - 7 < CHUNKS:
            return_z(t - 7)
        if t == CHUNKS:
            attend_end()
    total = final_own[...]
    for o in PLACE:
        if o:
            k = PLACE[o]
            last_z(o).wait_recv()
            total = total + last_got[k].astype(F32)
    finals[x] = total.astype(BF16)
    for d in (1, 3, 2):
        out_copy(d).start()
    for d in (1, 3, 2):
        out_copy_in(d).wait_recv()
    for i in range(X):
        out_ref[:, i * QUARTER : (i + 1) * QUARTER] = finals[i]

    for d in (1, 2, 3):
        att_copy(d).wait_send()
        att_top_copy(d).wait_send()
        out_copy(d).wait_send()
        for k in range(CHUNKS):
            sums_copy(k, d).wait_send()
            act_copy(k, d).wait_send()
            back_y(k, d).wait_send()
        for o in PLACE:
            fan(o, d).wait_send()
    for o in PLACE:
        if o:
            last_z(o).wait_send()
    spread(4).wait_send()
    for k in range(CHUNKS):
        pass_on(k).wait_send()
        give(k).wait_send()


def shards(query, cache, lengths, blocks, moe_tokens, routes, route_weights, w_gate, w_up, w_down):
    smem = pl.BlockSpec(memory_space=pltpu.SMEM)
    vmem = pl.BlockSpec(memory_space=pltpu.VMEM)
    hbm = pl.BlockSpec(memory_space=pl.ANY)
    scratch = lambda *shape: pltpu.VMEM(shape, BF16)
    wide = lambda *shape: pltpu.VMEM(shape, F32)
    return pl.pallas_call(
        kernel,
        out_shape=(
            jax.ShapeDtypeStruct((2, HEAD_SHARE, KV), BF16),
            jax.ShapeDtypeStruct((ROWS, X * QUARTER), BF16),
        ),
        in_specs=[smem, smem, vmem, vmem] + [hbm] * 6,
        out_specs=(vmem, vmem),
        scratch_shapes=[
            scratch(ROWS, WIDE),
            scratch(CHUNKS, Y, 2, ROWS, WIDE),
            scratch(QUARTER, UNITS),
            scratch(QUARTER, UNITS),
            scratch(UNITS, QUARTER),
            scratch(2, WIDTH, HEADS),
            scratch(2, WIDTH, SPAN),
            wide(X, 2, HEAD_SHARE, KV),
            scratch(X, 2, HEAD_SHARE, KV),
            wide(X, 2, HEAD_SHARE, 128),
            scratch(3, 2, HEAD_SHARE, KV),
            wide(3, 2, HEAD_SHARE, 128),
            scratch(CHUNK_ROWS, CHUNK_ROWS),
            scratch(CHUNKS, CHUNK_ROWS, SLOTS),
            wide(CHUNKS, CHUNK_ROWS, 128),
            wide(CHUNKS, X, SLOTS, 2 * SHARE),
            scratch(CHUNKS, X, SLOTS, 2 * SHARE),
            scratch(CHUNKS, 3, SLOTS, 2 * SHARE),
            scratch(CHUNKS, X, SLOTS, SHARE),
            wide(CHUNKS, Y, 2, ROWS, QUARTER),
            wide(CHUNKS, Y, ROWS, QUARTER),
            wide(CHUNKS, Y, ROWS, QUARTER),
            scratch(CHUNKS, Y, ROWS, QUARTER),
            scratch(CHUNKS, 3, ROWS, QUARTER),
            wide(ROWS, QUARTER),
            scratch(CHUNKS, ROWS, QUARTER),
            scratch(CHUNKS, ROWS, QUARTER),
            scratch(X, ROWS, QUARTER),
            pltpu.SemaphoreType.DMA((7,)),
            pltpu.SemaphoreType.DMA((len(COPIES),)),
            pltpu.SemaphoreType.DMA((len(COPIES),)),
        ],
        compiler_params=pltpu.CompilerParams(
            collective_id=0, has_side_effects=True, vmem_limit_bytes=62 * 1024 * 1024
        ),
    )(
        blocks, lengths, routes.T, route_weights.T, moe_tokens, jnp.swapaxes(query, 1, 2), jnp.swapaxes(cache, 1, 2),
        w_gate, w_up, w_down,
    )


def solution(mesh):
    return jax.shard_map(
        shards,
        mesh=mesh,
        in_specs=(
            P("expert", None, None),
            P("expert", "ctx", None),
            P("expert"),
            P("expert", None),
            P("expert", None),
            P("expert", None),
            P("expert", None),
            P("ctx", "expert"),
            P("ctx", "expert"),
            P("expert", "ctx"),
        ),
        out_specs=(P("expert", "ctx", None), P("expert", None)),
        check_vma=False,
    )
```

```python
import jax
import jax.numpy as jnp
from jax import lax
from jax.experimental import pallas as pl
from jax.experimental.pallas import tpu as pltpu
from jax.sharding import PartitionSpec as P

FF = 2048
KV = 512
QK_DIM = 192
EXPERTS = 16
BLOCK = 64
CAP = 12
Z, Y, X = 8, 4, 4
ROWS = 16
QUARTER = 1792
WIDE = QUARTER + 128
UNITS = 512
SLOTS = Y * 2 * CAP
SHARE = UNITS // X
SPAN = 2048
HEADS = 128
HEAD_SHARE = HEADS // X
WIDTH = 576
LOW = -1e30
PLANES = (0, 1, -1, 2, -2, 3, -3, 4)
CHUNKS = len(PLANES)
PLACE = {o: k for k, o in enumerate(PLANES)}
CHUNK_ROWS = Y * 2 * ROWS
F32 = jnp.float32
BF16 = jnp.bfloat16

COPIES = {}


def number(*key):
    return COPIES.setdefault(key, len(COPIES))


for d in (1, 2, 3):
    number("att", d)
    number("att_top", d)
    number("out", d)
    for k in range(CHUNKS):
        number("sums", k, d)
        number("act", k, d)
        number("back_y", k, d)
    for o in PLACE:
        number("fan", o, d)
for o in PLACE:
    if o:
        number("spread", o)
        number("last_z", o)
for k in range(CHUNKS):
    number("pass", k)
    number("give", k)


def kernel(
    blocks_ref, lengths_ref, routes_ref, route_weights_ref, tokens_hbm, query_hbm, cache_hbm, gate_hbm, up_hbm, down_hbm,
    att_ref, out_ref,
    own, rows_all, w_gate, w_up, w_down, query, cache,
    att_sum, att_send, att_top, att_got, att_got_top,
    earlier, place, mix, sums, sums_send, sums_got, acts,
    results, given, chips, chips_send, chips_got, final_own, last_send, last_got, finals,
    load_sem, send_sem, recv_sem,
):
    index = lax.axis_index("expert")
    x = lax.axis_index("ctx")
    core = lax.rem(index, 2)
    y = lax.rem(index // 2, Y)
    z = index // (2 * Y)
    own_expert = index // (FF // UNITS)

    def at(zz, yy, cc):
        return (zz * (2 * Y) + yy * 2 + cc, x)

    def zo(o):
        return lax.rem(z + o + Z, Z)

    def yo(o):
        return lax.rem(y + o + Y, Y)

    def xo(o):
        return lax.rem(x + o + X, X)

    def copy(key, src, dst, device):
        i = COPIES[key]
        return pltpu.make_async_remote_copy(
            src_ref=src, dst_ref=dst, send_sem=send_sem.at[i], recv_sem=recv_sem.at[i], device_id=device,
            device_id_type=pl.DeviceIdType.MESH,
        )

    to_y = lambda o: at(z, yo(o), core)
    to_z = lambda o: at(zo(o), y, core)
    to_x = lambda o: (index, xo(o))
    sibling = at(z, y, 1 - core)

    def load(i, src, dst):
        return pltpu.make_async_copy(src, dst, load_sem.at[i])

    loads = [
        load(0, tokens_hbm.at[:, pl.ds(pl.multiple_of(x * QUARTER, 128), QUARTER)], own.at[:, pl.ds(0, QUARTER)]),
        load(1, query_hbm, query),
        load(2, cache_hbm.at[0], cache.at[0]),
        load(3, cache_hbm.at[1], cache.at[1]),
        load(4, gate_hbm, w_gate),
        load(5, up_hbm, w_up),
        load(6, down_hbm, w_down),
    ]
    for one in loads:
        one.start()

    barrier = pltpu.get_barrier_semaphore()

    def greet(device):
        pl.semaphore_signal(barrier, inc=1, device_id=device, device_id_type=pl.DeviceIdType.MESH)

    for d in (1, 2, 3):
        greet(to_x(d))
        greet(to_y(d))
    greet(sibling)

    for d in range(1, Z):
        greet(to_z(d))

    expert_id = lax.broadcasted_iota(jnp.int32, (EXPERTS, ROWS), 0)
    mixing = jnp.zeros((EXPERTS, ROWS), F32)
    for k in range(8):
        mixing = jnp.where(expert_id == routes_ref[k : k + 1, :], route_weights_ref[k : k + 1, :], mixing)
    high = mixing.astype(BF16)
    low = (mixing - high.astype(F32)).astype(BF16)
    to_row = lax.broadcasted_iota(jnp.int32, (EXPERTS, 128), 0)
    to_lane = lax.broadcasted_iota(jnp.int32, (EXPERTS, 128), 1)
    turned = [
        lax.dot_general(
            part, jnp.where(to_lane == to_row + shift, 1.0, 0.0).astype(BF16), (((0,), (0,)), ((), ())),
            preferred_element_type=F32,
        )
        for part, shift in ((high, 0), (low, EXPERTS))
    ]
    own[:, QUARTER:] = (turned[0] + turned[1]).astype(BF16)
    row_id = lax.broadcasted_iota(jnp.int32, (CHUNK_ROWS, CHUNK_ROWS), 0)
    column_id = lax.broadcasted_iota(jnp.int32, (CHUNK_ROWS, CHUNK_ROWS), 1)
    earlier[...] = jnp.where((row_id // ROWS == column_id // ROWS) & (column_id < row_id), 1.0, 0.0).astype(BF16)
    loads[0].wait()

    rows_all[0, y, core] = own[...]
    pl.semaphore_wait(barrier, 14)

    def spread(o):
        k = PLACE[o]
        return copy(("spread", o), own, rows_all.at[k, y, core], to_z(-o))

    def fan(o, d):
        k = PLACE[o]
        return copy(("fan", o, d), rows_all.at[k, y, core], rows_all.at[k, y, core], to_y(d))

    def fan_in(o, d):
        k = PLACE[o]
        return copy(("fan", o, d), rows_all.at[k, yo(-d), core], rows_all.at[k, yo(-d), core], to_y(d))

    def pass_on(k):
        return copy(("pass", k), rows_all.at[k, :, core], rows_all.at[k, :, core], sibling)

    def pass_in(k):
        return copy(("pass", k), rows_all.at[k, :, 1 - core], rows_all.at[k, :, 1 - core], sibling)

    def fan_out(k):
        o = PLANES[k]
        if o:
            spread(o).wait_recv()
        for d in (1, 3, 2):
            fan(o, d).start()

    def gather(k):
        for d in (1, 3, 2):
            fan_in(PLANES[k], d).wait_recv()
        pass_on(k).start()

    fan_out(0)
    spread(1).start()
    spread(-1).start()

    def attend(s):
        position = x * SPAN + lax.broadcasted_iota(jnp.int32, (1, SPAN), 1)
        owning = position // BLOCK
        chosen = owning == blocks_ref[s, 0]
        for i in range(1, 32):
            chosen = chosen | (owning == blocks_ref[s, i])
        chosen = chosen & (position < lengths_ref[s])
        scores = lax.dot_general(query[s], cache[s], (((0,), (0,)), ((), ())), preferred_element_type=F32)
        scores = jnp.where(chosen, scores * QK_DIM ** (-0.5), LOW)
        peak = jnp.max(scores, axis=1, keepdims=True)
        weights = jnp.exp(scores - peak)
        total = jnp.sum(weights, axis=1, keepdims=True)
        latent = lax.dot_general(
            weights.astype(BF16), cache[s, :KV], (((1,), (1,)), ((), ())), preferred_element_type=F32
        )
        half = lax.broadcasted_iota(jnp.int32, (HEADS, 128), 1) < 64
        top = jnp.where(half, peak, total)
        for i in range(X):
            part = slice(i * HEAD_SHARE, (i + 1) * HEAD_SHARE)
            att_sum[i, s] = latent[part]
            att_send[i, s] = latent[part].astype(BF16)
            att_top[i, s] = top[part]

    def att_copy(d):
        return copy(("att", d), att_send.at[xo(d)], att_got.at[d - 1], to_x(d))

    def att_top_copy(d):
        return copy(("att_top", d), att_top.at[xo(d)], att_got_top.at[d - 1], to_x(d))

    def attend_end():
        for d in (1, 2, 3):
            att_copy(d).wait_recv()
            att_top_copy(d).wait_recv()
        tops = [att_top[x]] + [att_got_top[i] for i in range(3)]
        parts = [att_sum[x]] + [att_got[i].astype(F32) for i in range(3)]
        peaks = [t[:, :, 0:1] for t in tops]
        highest = jnp.maximum(jnp.maximum(peaks[0], peaks[1]), jnp.maximum(peaks[2], peaks[3]))
        factors = [jnp.exp(p - highest) for p in peaks]
        total = sum(f * t[:, :, 64:65] for f, t in zip(factors, tops))
        whole = sum(f * p for f, p in zip(factors, parts))
        att_ref[...] = (whole / total).astype(BF16)

    def chunk(k):
        pass_in(k).wait_recv()
        rows = rows_all[k].reshape(CHUNK_ROWS, WIDE)
        coefficients = rows[:, QUARTER:].astype(F32)
        lanes = lax.broadcasted_iota(jnp.int32, (CHUNK_ROWS, 128), 1)
        mine = (lanes == own_expert) | (lanes == own_expert + EXPERTS)
        share = jnp.sum(jnp.where(mine, coefficients, 0.0), axis=1, keepdims=True)
        hit = share > 0
        hits = jnp.broadcast_to(jnp.where(hit, 1.0, 0.0), (CHUNK_ROWS, 128)).astype(BF16)
        rank = jnp.dot(earlier[...], hits, preferred_element_type=F32)[:, :1].astype(jnp.int32)
        slot = rank + CAP * (lax.broadcasted_iota(jnp.int32, (CHUNK_ROWS, 1), 0) // ROWS)
        slot = jnp.where(hit, slot, -1)
        placing = jnp.where(slot == lax.broadcasted_iota(jnp.int32, (CHUNK_ROWS, SLOTS), 1), 1.0, 0.0).astype(BF16)
        place[k] = placing
        mix[k] = jnp.broadcast_to(share, (CHUNK_ROWS, 128))
        packed = lax.dot_general(
            placing, rows[:, :QUARTER], (((0,), (0,)), ((), ())), preferred_element_type=F32
        ).astype(BF16)
        for half, weight in enumerate((w_gate, w_up)):
            part = jnp.dot(packed, weight[...], preferred_element_type=F32)
            for i in range(X):
                one = part[:, i * SHARE : (i + 1) * SHARE]
                sums[k, i, :, half * SHARE : (half + 1) * SHARE] = one
                sums_send[k, i, :, half * SHARE : (half + 1) * SHARE] = one.astype(BF16)
        for d in (1, 3, 2):
            sums_copy(k, d).start()

    def sums_copy(k, d):
        return copy(("sums", k, d), sums_send.at[k, xo(d)], sums_got.at[k, d - 1], to_x(d))

    def act_copy(k, d):
        return copy(("act", k, d), acts.at[k, x], acts.at[k, x], to_x(d))

    def act_copy_in(k, d):
        return copy(("act", k, d), acts.at[k, xo(-d)], acts.at[k, xo(-d)], to_x(d))

    def activate(k):
        for d in (1, 2, 3):
            sums_copy(k, d).wait_recv()
        both = sums[k, x]
        for i in range(3):
            both = both + sums_got[k, i].astype(F32)
        gate, up = both[:, :SHARE], both[:, SHARE:]
        acts[k, x] = (gate / (1.0 + jnp.exp(-gate)) * up).astype(BF16)
        for d in (1, 3, 2):
            act_copy(k, d).start()

    def give(k):
        return copy(("give", k), results.at[k, :, 1 - core], given.at[k], sibling)

    def finish(k):
        for d in (1, 2, 3):
            act_copy_in(k, d).wait_recv()
        inside = jnp.concatenate([acts[k, i] for i in range(X)], axis=1)
        spread_out = jnp.dot(place[k], inside, preferred_element_type=F32).astype(BF16)
        result = jnp.dot(spread_out, w_down[...], preferred_element_type=F32) * mix[k][:, :1]
        results[k] = result.reshape(Y, 2, ROWS, QUARTER)
        give(k).start()

    def back_y(k, d):
        return copy(("back_y", k, d), chips_send.at[k, yo(d)], chips_got.at[k, d - 1], to_y(d))

    def last_z(o):
        k = PLACE[o]
        return copy(("last_z", o), last_send.at[k], last_got.at[k], to_z(o))

    def out_copy(d):
        return copy(("out", d), finals.at[x], finals.at[x], to_x(d))

    def out_copy_in(d):
        return copy(("out", d), finals.at[xo(-d)], finals.at[xo(-d)], to_x(d))

    def return_y(k):
        give(k).wait_recv()
        for j in range(Y):
            one = results[k, j, core] + given[k, j]
            chips[k, j] = one
            chips_send[k, j] = one.astype(BF16)
        for d in (1, 3, 2):
            back_y(k, d).start()

    def return_z(k):
        for d in (1, 3, 2):
            back_y(k, d).wait_recv()
        one = chips[k, y]
        for j in range(3):
            one = one + chips_got[k, j].astype(F32)
        if k:
            last_send[k] = one.astype(BF16)
            last_z(PLANES[k]).start()
        else:
            final_own[...] = one

    def spread_next(sent, following):
        for o in sent:
            spread(o).wait_send()
        for o in following:
            spread(o).start()

    loads[1].wait()
    loads[2].wait()
    attend(0)
    spread_next((1, -1), (2, -2))
    fan_out(1)
    fan_out(2)
    loads[3].wait()
    attend(1)
    for d in (1, 3, 2):
        att_copy(d).start()
        att_top_copy(d).start()
    spread_next((2, -2), (3, -3))
    gather(0)
    loads[4].wait()
    loads[5].wait()
    for t in range(CHUNKS + 8):
        if t + 3 < CHUNKS:
            fan_out(t + 3)
        if t == 0:
            spread_next((3, -3), (4,))
        if t + 1 < CHUNKS:
            gather(t + 1)
        if t < CHUNKS:
            chunk(t)
        if t == 3:
            loads[6].wait()
        if 0 <= t - 3 < CHUNKS:
            activate(t - 3)
        if 0 <= t - 5 < CHUNKS:
            finish(t - 5)
        if 0 <= t - 6 < CHUNKS:
            return_y(t - 6)
        if 0 <= t - 8 < CHUNKS:
            return_z(t - 8)
        if t == CHUNKS:
            attend_end()
    total = final_own[...]
    for o in PLACE:
        if o:
            k = PLACE[o]
            last_z(o).wait_recv()
            total = total + last_got[k].astype(F32)
    finals[x] = total.astype(BF16)
    for d in (1, 3, 2):
        out_copy(d).start()
    for d in (1, 3, 2):
        out_copy_in(d).wait_recv()
    for i in range(X):
        out_ref[:, i * QUARTER : (i + 1) * QUARTER] = finals[i]

    for d in (1, 2, 3):
        att_copy(d).wait_send()
        att_top_copy(d).wait_send()
        out_copy(d).wait_send()
        for k in range(CHUNKS):
            sums_copy(k, d).wait_send()
            act_copy(k, d).wait_send()
            back_y(k, d).wait_send()
        for o in PLACE:
            fan(o, d).wait_send()
    for o in PLACE:
        if o:
            last_z(o).wait_send()
    spread(4).wait_send()
    for k in range(CHUNKS):
        pass_on(k).wait_send()
        give(k).wait_send()


def shards(query, cache, lengths, blocks, moe_tokens, routes, route_weights, w_gate, w_up, w_down):
    smem = pl.BlockSpec(memory_space=pltpu.SMEM)
    vmem = pl.BlockSpec(memory_space=pltpu.VMEM)
    hbm = pl.BlockSpec(memory_space=pl.ANY)
    scratch = lambda *shape: pltpu.VMEM(shape, BF16)
    wide = lambda *shape: pltpu.VMEM(shape, F32)
    return pl.pallas_call(
        kernel,
        out_shape=(
            jax.ShapeDtypeStruct((2, HEAD_SHARE, KV), BF16),
            jax.ShapeDtypeStruct((ROWS, X * QUARTER), BF16),
        ),
        in_specs=[smem, smem, vmem, vmem] + [hbm] * 6,
        out_specs=(vmem, vmem),
        scratch_shapes=[
            scratch(ROWS, WIDE),
            scratch(CHUNKS, Y, 2, ROWS, WIDE),
            scratch(QUARTER, UNITS),
            scratch(QUARTER, UNITS),
            scratch(UNITS, QUARTER),
            scratch(2, WIDTH, HEADS),
            scratch(2, WIDTH, SPAN),
            wide(X, 2, HEAD_SHARE, KV),
            scratch(X, 2, HEAD_SHARE, KV),
            wide(X, 2, HEAD_SHARE, 128),
            scratch(3, 2, HEAD_SHARE, KV),
            wide(3, 2, HEAD_SHARE, 128),
            scratch(CHUNK_ROWS, CHUNK_ROWS),
            scratch(CHUNKS, CHUNK_ROWS, SLOTS),
            wide(CHUNKS, CHUNK_ROWS, 128),
            wide(CHUNKS, X, SLOTS, 2 * SHARE),
            scratch(CHUNKS, X, SLOTS, 2 * SHARE),
            scratch(CHUNKS, 3, SLOTS, 2 * SHARE),
            scratch(CHUNKS, X, SLOTS, SHARE),
            wide(CHUNKS, Y, 2, ROWS, QUARTER),
            wide(CHUNKS, Y, ROWS, QUARTER),
            wide(CHUNKS, Y, ROWS, QUARTER),
            scratch(CHUNKS, Y, ROWS, QUARTER),
            scratch(CHUNKS, 3, ROWS, QUARTER),
            wide(ROWS, QUARTER),
            scratch(CHUNKS, ROWS, QUARTER),
            scratch(CHUNKS, ROWS, QUARTER),
            scratch(X, ROWS, QUARTER),
            pltpu.SemaphoreType.DMA((7,)),
            pltpu.SemaphoreType.DMA((len(COPIES),)),
            pltpu.SemaphoreType.DMA((len(COPIES),)),
        ],
        compiler_params=pltpu.CompilerParams(
            collective_id=0, has_side_effects=True, vmem_limit_bytes=62 * 1024 * 1024
        ),
    )(
        blocks, lengths, routes.T, route_weights.T, moe_tokens, jnp.swapaxes(query, 1, 2), jnp.swapaxes(cache, 1, 2),
        w_gate, w_up, w_down,
    )


def solution(mesh):
    return jax.shard_map(
        shards,
        mesh=mesh,
        in_specs=(
            P("expert", None, None),
            P("expert", "ctx", None),
            P("expert"),
            P("expert", None),
            P("expert", None),
            P("expert", None),
            P("expert", None),
            P("ctx", "expert"),
            P("ctx", "expert"),
            P("expert", "ctx"),
        ),
        out_specs=(P("expert", "ctx", None), P("expert", None)),
        check_vma=False,
    )
```

```python
import jax
import jax.numpy as jnp
from jax import lax
from jax.experimental import pallas as pl
from jax.experimental.pallas import tpu as pltpu
from jax.sharding import PartitionSpec as P

FF = 2048
KV = 512
QK_DIM = 192
EXPERTS = 16
BLOCK = 64
CAP = 12
Z, Y, X = 8, 4, 4
ROWS = 16
QUARTER = 1792
WIDE = QUARTER + 128
UNITS = 512
SLOTS = Y * 2 * CAP
SHARE = UNITS // X
SPAN = 2048
HEADS = 128
HEAD_SHARE = HEADS // X
WIDTH = 576
LOW = -1e30
PLANES = (0, 1, -1, 2, -2, 3, -3, 4)
CHUNKS = len(PLANES)
PLACE = {o: k for k, o in enumerate(PLANES)}
CHUNK_ROWS = Y * 2 * ROWS
F32 = jnp.float32
BF16 = jnp.bfloat16

COPIES = {}


def number(*key):
    return COPIES.setdefault(key, len(COPIES))


for d in (1, 2, 3):
    number("att", d)
    number("att_top", d)
    number("out", d)
    for k in range(CHUNKS):
        number("sums", k, d)
        number("act", k, d)
        number("back_y", k, d)
    for o in PLACE:
        number("fan", o, d)
for o in PLACE:
    if o:
        number("spread", o)
        number("last_z", o)
for k in range(CHUNKS):
    number("pass", k)
    number("give", k)


def kernel(
    blocks_ref, lengths_ref, routes_ref, route_weights_ref, tokens_hbm, query_hbm, cache_hbm, gate_hbm, up_hbm, down_hbm,
    att_ref, out_ref,
    own, rows_all, w_gate, w_up, w_down, query, cache,
    att_sum, att_send, att_top, att_got, att_got_top,
    earlier, place, mix, sums, sums_send, sums_got, acts,
    results, given, chips, chips_send, chips_got, final_own, last_send, last_got, finals,
    load_sem, send_sem, recv_sem,
):
    index = lax.axis_index("expert")
    x = lax.axis_index("ctx")
    core = lax.rem(index, 2)
    y = lax.rem(index // 2, Y)
    z = index // (2 * Y)
    own_expert = index // (FF // UNITS)

    def at(zz, yy, cc):
        return (zz * (2 * Y) + yy * 2 + cc, x)

    def zo(o):
        return lax.rem(z + o + Z, Z)

    def yo(o):
        return lax.rem(y + o + Y, Y)

    def xo(o):
        return lax.rem(x + o + X, X)

    def copy(key, src, dst, device):
        i = COPIES[key]
        return pltpu.make_async_remote_copy(
            src_ref=src, dst_ref=dst, send_sem=send_sem.at[i], recv_sem=recv_sem.at[i], device_id=device,
            device_id_type=pl.DeviceIdType.MESH,
        )

    to_y = lambda o: at(z, yo(o), core)
    to_z = lambda o: at(zo(o), y, core)
    to_x = lambda o: (index, xo(o))
    sibling = at(z, y, 1 - core)

    def load(i, src, dst):
        return pltpu.make_async_copy(src, dst, load_sem.at[i])

    loads = [
        load(0, tokens_hbm.at[:, pl.ds(pl.multiple_of(x * QUARTER, 128), QUARTER)], own.at[:, pl.ds(0, QUARTER)]),
        load(1, query_hbm, query),
        load(2, cache_hbm.at[0], cache.at[0]),
        load(3, cache_hbm.at[1], cache.at[1]),
        load(4, gate_hbm, w_gate),
        load(5, up_hbm, w_up),
        load(6, down_hbm, w_down),
    ]
    for one in loads:
        one.start()

    barrier = pltpu.get_barrier_semaphore()

    def greet(device):
        pl.semaphore_signal(barrier, inc=1, device_id=device, device_id_type=pl.DeviceIdType.MESH)

    for d in (1, 2, 3):
        greet(to_x(d))
        greet(to_y(d))
    greet(sibling)

    for d in range(1, Z):
        greet(to_z(d))

    expert_id = lax.broadcasted_iota(jnp.int32, (EXPERTS, ROWS), 0)
    mixing = jnp.zeros((EXPERTS, ROWS), F32)
    for k in range(8):
        mixing = jnp.where(expert_id == routes_ref[k : k + 1, :], route_weights_ref[k : k + 1, :], mixing)
    high = mixing.astype(BF16)
    low = (mixing - high.astype(F32)).astype(BF16)
    to_row = lax.broadcasted_iota(jnp.int32, (EXPERTS, 128), 0)
    to_lane = lax.broadcasted_iota(jnp.int32, (EXPERTS, 128), 1)
    turned = [
        lax.dot_general(
            part, jnp.where(to_lane == to_row + shift, 1.0, 0.0).astype(BF16), (((0,), (0,)), ((), ())),
            preferred_element_type=F32,
        )
        for part, shift in ((high, 0), (low, EXPERTS))
    ]
    own[:, QUARTER:] = (turned[0] + turned[1]).astype(BF16)
    row_id = lax.broadcasted_iota(jnp.int32, (CHUNK_ROWS, CHUNK_ROWS), 0)
    column_id = lax.broadcasted_iota(jnp.int32, (CHUNK_ROWS, CHUNK_ROWS), 1)
    earlier[...] = jnp.where((row_id // ROWS == column_id // ROWS) & (column_id < row_id), 1.0, 0.0).astype(BF16)
    loads[0].wait()

    rows_all[0, y, core] = own[...]
    pl.semaphore_wait(barrier, 14)

    def spread(o):
        k = PLACE[o]
        return copy(("spread", o), own, rows_all.at[k, y, core], to_z(-o))

    def fan(o, d):
        k = PLACE[o]
        return copy(("fan", o, d), rows_all.at[k, y, core], rows_all.at[k, y, core], to_y(d))

    def fan_in(o, d):
        k = PLACE[o]
        return copy(("fan", o, d), rows_all.at[k, yo(-d), core], rows_all.at[k, yo(-d), core], to_y(d))

    def pass_on(k):
        return copy(("pass", k), rows_all.at[k, :, core], rows_all.at[k, :, core], sibling)

    def pass_in(k):
        return copy(("pass", k), rows_all.at[k, :, 1 - core], rows_all.at[k, :, 1 - core], sibling)

    def fan_out(k):
        o = PLANES[k]
        if o:
            spread(o).wait_recv()
        for d in (1, 3, 2):
            fan(o, d).start()

    def gather(k):
        for d in (1, 3, 2):
            fan_in(PLANES[k], d).wait_recv()
        pass_on(k).start()

    fan_out(0)
    spread(1).start()
    spread(-1).start()

    def attend(s):
        position = x * SPAN + lax.broadcasted_iota(jnp.int32, (1, SPAN), 1)
        owning = position // BLOCK
        chosen = owning == blocks_ref[s, 0]
        for i in range(1, 32):
            chosen = chosen | (owning == blocks_ref[s, i])
        chosen = chosen & (position < lengths_ref[s])
        scores = lax.dot_general(query[s], cache[s], (((0,), (0,)), ((), ())), preferred_element_type=F32)
        scores = jnp.where(chosen, scores * QK_DIM ** (-0.5), LOW)
        peak = jnp.max(scores, axis=1, keepdims=True)
        weights = jnp.exp(scores - peak)
        total = jnp.sum(weights, axis=1, keepdims=True)
        latent = lax.dot_general(
            weights.astype(BF16), cache[s, :KV], (((1,), (1,)), ((), ())), preferred_element_type=F32
        )
        half = lax.broadcasted_iota(jnp.int32, (HEADS, 128), 1) < 64
        top = jnp.where(half, peak, total)
        for i in range(X):
            part = slice(i * HEAD_SHARE, (i + 1) * HEAD_SHARE)
            att_sum[i, s] = latent[part]
            att_send[i, s] = latent[part].astype(BF16)
            att_top[i, s] = top[part]

    def att_copy(d):
        return copy(("att", d), att_send.at[xo(d)], att_got.at[d - 1], to_x(d))

    def att_top_copy(d):
        return copy(("att_top", d), att_top.at[xo(d)], att_got_top.at[d - 1], to_x(d))

    def attend_end():
        for d in (1, 2, 3):
            att_copy(d).wait_recv()
            att_top_copy(d).wait_recv()
        tops = [att_top[x]] + [att_got_top[i] for i in range(3)]
        parts = [att_sum[x]] + [att_got[i].astype(F32) for i in range(3)]
        peaks = [t[:, :, 0:1] for t in tops]
        highest = jnp.maximum(jnp.maximum(peaks[0], peaks[1]), jnp.maximum(peaks[2], peaks[3]))
        factors = [jnp.exp(p - highest) for p in peaks]
        total = sum(f * t[:, :, 64:65] for f, t in zip(factors, tops))
        whole = sum(f * p for f, p in zip(factors, parts))
        att_ref[...] = (whole / total).astype(BF16)

    def chunk(k):
        pass_in(k).wait_recv()
        rows = rows_all[k].reshape(CHUNK_ROWS, WIDE)
        coefficients = rows[:, QUARTER:].astype(F32)
        lanes = lax.broadcasted_iota(jnp.int32, (CHUNK_ROWS, 128), 1)
        mine = (lanes == own_expert) | (lanes == own_expert + EXPERTS)
        share = jnp.sum(jnp.where(mine, coefficients, 0.0), axis=1, keepdims=True)
        hit = share > 0
        hits = jnp.broadcast_to(jnp.where(hit, 1.0, 0.0), (CHUNK_ROWS, 128)).astype(BF16)
        rank = jnp.dot(earlier[...], hits, preferred_element_type=F32)[:, :1].astype(jnp.int32)
        slot = rank + CAP * (lax.broadcasted_iota(jnp.int32, (CHUNK_ROWS, 1), 0) // ROWS)
        slot = jnp.where(hit, slot, -1)
        placing = jnp.where(slot == lax.broadcasted_iota(jnp.int32, (CHUNK_ROWS, SLOTS), 1), 1.0, 0.0).astype(BF16)
        place[k] = placing
        mix[k] = jnp.broadcast_to(share, (CHUNK_ROWS, 128))
        packed = lax.dot_general(
            placing, rows[:, :QUARTER], (((0,), (0,)), ((), ())), preferred_element_type=F32
        ).astype(BF16)
        for half, weight in enumerate((w_gate, w_up)):
            part = jnp.dot(packed, weight[...], preferred_element_type=F32)
            for i in range(X):
                one = part[:, i * SHARE : (i + 1) * SHARE]
                sums[k, i, :, half * SHARE : (half + 1) * SHARE] = one
                sums_send[k, i, :, half * SHARE : (half + 1) * SHARE] = one.astype(BF16)
        for d in (1, 3, 2):
            sums_copy(k, d).start()

    def sums_copy(k, d):
        return copy(("sums", k, d), sums_send.at[k, xo(d)], sums_got.at[k, d - 1], to_x(d))

    def act_copy(k, d):
        return copy(("act", k, d), acts.at[k, x], acts.at[k, x], to_x(d))

    def act_copy_in(k, d):
        return copy(("act", k, d), acts.at[k, xo(-d)], acts.at[k, xo(-d)], to_x(d))

    def activate(k):
        for d in (1, 2, 3):
            sums_copy(k, d).wait_recv()
        both = sums[k, x]
        for i in range(3):
            both = both + sums_got[k, i].astype(F32)
        gate, up = both[:, :SHARE], both[:, SHARE:]
        acts[k, x] = (gate / (1.0 + jnp.exp(-gate)) * up).astype(BF16)
        for d in (1, 3, 2):
            act_copy(k, d).start()

    def give(k):
        return copy(("give", k), results.at[k, :, 1 - core], given.at[k], sibling)

    def finish(k):
        for d in (1, 2, 3):
            act_copy_in(k, d).wait_recv()
        inside = jnp.concatenate([acts[k, i] for i in range(X)], axis=1)
        spread_out = jnp.dot(place[k], inside, preferred_element_type=F32).astype(BF16)
        result = jnp.dot(spread_out, w_down[...], preferred_element_type=F32) * mix[k][:, :1]
        results[k] = result.reshape(Y, 2, ROWS, QUARTER)
        give(k).start()

    def back_y(k, d):
        return copy(("back_y", k, d), chips_send.at[k, yo(d)], chips_got.at[k, d - 1], to_y(d))

    def last_z(o):
        k = PLACE[o]
        return copy(("last_z", o), last_send.at[k], last_got.at[k], to_z(o))

    def out_copy(d):
        return copy(("out", d), finals.at[x], finals.at[x], to_x(d))

    def out_copy_in(d):
        return copy(("out", d), finals.at[xo(-d)], finals.at[xo(-d)], to_x(d))

    def return_y(k):
        give(k).wait_recv()
        for j in range(Y):
            one = results[k, j, core] + given[k, j]
            chips[k, j] = one
            chips_send[k, j] = one.astype(BF16)
        for d in (1, 3, 2):
            back_y(k, d).start()

    def return_z(k):
        for d in (1, 3, 2):
            back_y(k, d).wait_recv()
        one = chips[k, y]
        for j in range(3):
            one = one + chips_got[k, j].astype(F32)
        if k:
            last_send[k] = one.astype(BF16)
            last_z(PLANES[k]).start()
        else:
            final_own[...] = one

    def spread_next(sent, following):
        for o in sent:
            spread(o).wait_send()
        for o in following:
            spread(o).start()

    loads[1].wait()
    loads[2].wait()
    attend(0)
    spread_next((1, -1), (2, -2))
    fan_out(1)
    fan_out(2)
    loads[3].wait()
    attend(1)
    for d in (1, 3, 2):
        att_copy(d).start()
        att_top_copy(d).start()
    spread_next((2, -2), (3, -3))
    gather(0)
    loads[4].wait()
    loads[5].wait()
    for t in range(CHUNKS + 7):
        if t + 3 < CHUNKS:
            fan_out(t + 3)
        if t == 0:
            spread_next((3, -3), (4,))
        if 0 <= t - 2 < CHUNKS:
            activate(t - 2)
        if t < CHUNKS:
            chunk(t)
        if t == 3:
            loads[6].wait()
        if 0 <= t - 4 < CHUNKS:
            finish(t - 4)
        if 0 <= t - 5 < CHUNKS:
            return_y(t - 5)
        if 0 <= t - 7 < CHUNKS:
            return_z(t - 7)
        if t == 4:
            attend_end()
        if t + 1 < CHUNKS:
            gather(t + 1)
    total = final_own[...]
    for o in PLACE:
        if o:
            k = PLACE[o]
            last_z(o).wait_recv()
            total = total + last_got[k].astype(F32)
    finals[x] = total.astype(BF16)
    for d in (1, 3, 2):
        out_copy(d).start()
    for d in (1, 3, 2):
        out_copy_in(d).wait_recv()
    for i in range(X):
        out_ref[:, i * QUARTER : (i + 1) * QUARTER] = finals[i]

    for d in (1, 2, 3):
        att_copy(d).wait_send()
        att_top_copy(d).wait_send()
        out_copy(d).wait_send()
        for k in range(CHUNKS):
            sums_copy(k, d).wait_send()
            act_copy(k, d).wait_send()
            back_y(k, d).wait_send()
        for o in PLACE:
            fan(o, d).wait_send()
    for o in PLACE:
        if o:
            last_z(o).wait_send()
    spread(4).wait_send()
    for k in range(CHUNKS):
        pass_on(k).wait_send()
        give(k).wait_send()


def shards(query, cache, lengths, blocks, moe_tokens, routes, route_weights, w_gate, w_up, w_down):
    smem = pl.BlockSpec(memory_space=pltpu.SMEM)
    vmem = pl.BlockSpec(memory_space=pltpu.VMEM)
    hbm = pl.BlockSpec(memory_space=pl.ANY)
    scratch = lambda *shape: pltpu.VMEM(shape, BF16)
    wide = lambda *shape: pltpu.VMEM(shape, F32)
    return pl.pallas_call(
        kernel,
        out_shape=(
            jax.ShapeDtypeStruct((2, HEAD_SHARE, KV), BF16),
            jax.ShapeDtypeStruct((ROWS, X * QUARTER), BF16),
        ),
        in_specs=[smem, smem, vmem, vmem] + [hbm] * 6,
        out_specs=(vmem, vmem),
        scratch_shapes=[
            scratch(ROWS, WIDE),
            scratch(CHUNKS, Y, 2, ROWS, WIDE),
            scratch(QUARTER, UNITS),
            scratch(QUARTER, UNITS),
            scratch(UNITS, QUARTER),
            scratch(2, WIDTH, HEADS),
            scratch(2, WIDTH, SPAN),
            wide(X, 2, HEAD_SHARE, KV),
            scratch(X, 2, HEAD_SHARE, KV),
            wide(X, 2, HEAD_SHARE, 128),
            scratch(3, 2, HEAD_SHARE, KV),
            wide(3, 2, HEAD_SHARE, 128),
            scratch(CHUNK_ROWS, CHUNK_ROWS),
            scratch(CHUNKS, CHUNK_ROWS, SLOTS),
            wide(CHUNKS, CHUNK_ROWS, 128),
            wide(CHUNKS, X, SLOTS, 2 * SHARE),
            scratch(CHUNKS, X, SLOTS, 2 * SHARE),
            scratch(CHUNKS, 3, SLOTS, 2 * SHARE),
            scratch(CHUNKS, X, SLOTS, SHARE),
            wide(CHUNKS, Y, 2, ROWS, QUARTER),
            wide(CHUNKS, Y, ROWS, QUARTER),
            wide(CHUNKS, Y, ROWS, QUARTER),
            scratch(CHUNKS, Y, ROWS, QUARTER),
            scratch(CHUNKS, 3, ROWS, QUARTER),
            wide(ROWS, QUARTER),
            scratch(CHUNKS, ROWS, QUARTER),
            scratch(CHUNKS, ROWS, QUARTER),
            scratch(X, ROWS, QUARTER),
            pltpu.SemaphoreType.DMA((7,)),
            pltpu.SemaphoreType.DMA((len(COPIES),)),
            pltpu.SemaphoreType.DMA((len(COPIES),)),
        ],
        compiler_params=pltpu.CompilerParams(
            collective_id=0, has_side_effects=True, vmem_limit_bytes=62 * 1024 * 1024
        ),
    )(
        blocks, lengths, routes.T, route_weights.T, moe_tokens, jnp.swapaxes(query, 1, 2), jnp.swapaxes(cache, 1, 2),
        w_gate, w_up, w_down,
    )


def solution(mesh):
    return jax.shard_map(
        shards,
        mesh=mesh,
        in_specs=(
            P("expert", None, None),
            P("expert", "ctx", None),
            P("expert"),
            P("expert", None),
            P("expert", None),
            P("expert", None),
            P("expert", None),
            P("ctx", "expert"),
            P("ctx", "expert"),
            P("expert", "ctx"),
        ),
        out_specs=(P("expert", "ctx", None), P("expert", None)),
        check_vma=False,
    )
```
